32 devices in a mesh: ex: 4 (over z), sh: 8 (over y, x, core).
Axes of the slice: x: 2, y: 2, z: 4, core: 2. Of those that a mesh axis runs over, the one named last changes fastest.
Arguments:
- hidden_in: bfloat16 [3072, 2304], P(('ex', 'sh')), may hold values from -3 to 3
- queries: bfloat16 [3072, 2304], P(('ex', 'sh')), may hold values from -2.5 to 2.5
- new_keys: bfloat16 [3072, 2304], P(('ex', 'sh')), may hold values from -2.5 to 2.5
- new_values: bfloat16 [3072, 2304], P(('ex', 'sh')), may hold values from -6 to 6
- key_pool: bfloat16 [32768, 2304], P(('ex', 'sh')), may hold values from -2.5 to 2.5
- value_pool: bfloat16 [32768, 2304], P(('ex', 'sh')), may hold values from -6 to 6
- page_order: int32 [32, 64], P(('ex', 'sh')), may hold values from 0 to 63, each once within a row
- new_lengths: int32 [32, 4], P(('ex', 'sh')), may hold values from 1 to 48, 96 in all within a row
- context_lengths: int32 [32, 4], P(('ex', 'sh')), may hold values from 1 to 256, 512 in all within a row
- route_ids: int32 [3072, 2], P(('ex', 'sh')), may hold values from 0 to 7, all different within a row; in each aligned block of 96 rows (0 to 95, 96 to 191, ...) at most 32 rows name the same one
- norm_gain: bfloat16 [2304], replicated, may hold values from 0.25 to 1.75
- router_weight: bfloat16 [2304, 8], replicated, may hold values from -0.125 to 0.125
- gate_weight: bfloat16 [8, 2304, 5760], P('ex', None, 'sh'), may hold values from -0.125 to 0.125
- up_weight: bfloat16 [8, 2304, 5760], P('ex', None, 'sh'), may hold values from -0.125 to 0.125
- down_weight: bfloat16 [8, 5760, 2304], P('ex', 'sh'), may hold values from -0.078125 to 0.078125
- out_gain: bfloat16 [2304], replicated, may hold values from 0.25 to 1.75
Outputs:
- layer_out: bfloat16 [3072, 2304], P(('ex', 'sh'))
The draws below stay inside these ranges and needn't reach their ends.
Inputs may be any that keep to these rules, and one draw needn't show every extreme that they name: `page_order`: each row names the pages 0 to 63 of one device's pool once each; request r owns entries r * 16 to (r+1) * 16 - 1 of its row, in order. `new_lengths`: each row sums to 96; its largest entry is 48. `context_lengths`: each row sums to 512; its largest entry is 256. `route_ids`: A row names two different experts. Among the 96 rows of one device no expert is named by more than 32 rows, and in some devices' rows one expert is named by exactly 32.
All inputs are finite; a program needn't handle non-finite values.
Results may differ from the reference program's by a relative error of at most 0.015.
Values may be sent and summed in bfloat16 or wider, within the bound.
A program may use at most 128 MiB of HBM per device.

```python
import math
import jax
import jax.numpy as jnp
import numpy as np
from jax import lax

D = 2304
HEADS = 36
HEAD_DIM = 64
FF = 5760
EXPERTS = 8
TOP = 2
TOK_DEV = 96
REQ_DEV = 4
PAGE = 16
PAGES_DEV = 64
BLOCKS = 32
TOKENS = 3072
POOL = 1024
CTX_MOST = 256
CTX_TOTAL = 512
NEW_MOST = 48
MOST = 32
FF_SLICE = 720
N_SH = 8


def steps_of(stream_key, shape, cuts, low, largest):
    factor_of, own = 1.0, jax.random.fold_in(stream_key, 6)
    for dim, parts in cuts:
        draws = jnp.exp(jax.random.uniform(jax.random.fold_in(own, dim), (parts,), jnp.float32, low / len(cuts), largest / len(cuts)))
        factor_of = factor_of * jnp.repeat(draws, shape[dim] // parts).reshape([-1 if axis == dim else 1 for axis in range(len(shape))])
    return factor_of


def split_up(amount, total, most, lean):
    weights = [(1 << 20) // math.isqrt(grade ** lean) + 1 for grade in range(2, amount + 1)]
    rest, counts = total - most - (amount - 1), [1] * (amount - 1)
    while rest > 0:
        movable = [i for i in range(amount - 1) if counts[i] < most]
        whole, budget = sum([weights[i] for i in movable]), rest
        for i in movable:
            more = min(most - counts[i], max(1, budget * weights[i] // whole), rest)
            counts[i] = counts[i] + more
            rest = rest - more
    return np.array([most] + counts)


def uneven_parts(key, amount, total, most, lean):
    if amount == 2:
        one = jax.random.randint(key, (), max(1, total - most), min(most, total - 1) + 1)
        return jnp.stack([one, total - one])
    sizes = jnp.asarray(split_up(amount, total, most, lean), jnp.int32)
    pairs = (amount - 1) // 2
    giver, sink = sizes[1:1 + 2 * pairs:2], sizes[2:2 + 2 * pairs:2]
    room = jnp.minimum(giver - 1, most - sink)
    moved = jax.random.randint(jax.random.fold_in(key, 1), (pairs,), 0, 1 << 20) % (room + 1)
    sizes = sizes.at[1:1 + 2 * pairs:2].set(giver - moved).at[2:2 + 2 * pairs:2].set(sink + moved)
    return sizes[jax.random.permutation(jax.random.fold_in(key, 2), amount)]


def shared_out(stream_key, own, number, rows, amount, top, limit, skew):
    sequence = jax.random.permutation(stream_key, amount)
    crowded, ordinary = load_shares(amount, rows * top, limit, skew, True), load_shares(amount, rows * top, limit, skew, False)
    places = jnp.arange(amount)

    def named(sizes, turn):
        used = int((sizes > 0).sum())
        fixed = max(1, used // 4)
        passed = fixed + (places - fixed + turn * (used - fixed)) % max(1, amount - fixed)
        return jnp.zeros((amount,), jnp.int32).at[sequence[jnp.where(places < fixed, places, passed)]].set(jnp.asarray(sizes, jnp.int32))

    sizes = jnp.where(number % 4 == 0, named(crowded, number // 4), named(ordinary, number - number // 4 - 1))
    mixed = jax.random.permutation(jax.random.fold_in(own, 3), amount)
    source_of, receiver = mixed[0:amount // 2 * 2:2], mixed[1:amount // 2 * 2:2]
    room = jnp.minimum(sizes[source_of] - 1, limit - sizes[receiver]) // 2
    room = jnp.where((source_of == sequence[0]) | (receiver == sequence[0]) | (sizes[receiver] == 0), 0, jnp.maximum(room, 0))
    passed = jax.random.randint(jax.random.fold_in(own, 4), (amount // 2,), 0, 1 << 20) % (room + 1)
    sizes = sizes.at[source_of].add(-passed).at[receiver].add(passed)
    members = jnp.searchsorted(jnp.cumsum(sizes), jnp.arange(rows * top), side="right").astype(jnp.int32)
    listing = members.reshape(top, rows).T
    listing = listing[jax.random.permutation(jax.random.fold_in(own, 1), rows)]
    turn = jax.random.randint(jax.random.fold_in(own, 2), (rows, 1), 0, top)
    return jnp.take_along_axis(listing, (jnp.arange(top)[None, :] + turn) % top, axis=1)


def load_shares(amount, total, reach, skew, full):
    portions = [(1 << 20) // math.isqrt(standing ** skew) + 1 for standing in range(1, amount + 1)]
    largest = reach if full else min(reach, max(-(-total // amount), total * portions[0] // sum(portions)))
    least = 1 if total - largest >= amount - 1 else 0
    given, spare = [largest] + [least] * (amount - 1), total - largest - least * (amount - 1)
    while spare > 0:
        free = [i for i in range(1, amount) if given[i] < largest] or [i for i in range(1, amount) if given[i] < reach]
        pool, left = sum([portions[i] for i in free]), spare
        for i in free:
            more = min(reach - given[i], max(1, left * portions[i] // pool), spare)
            given[i] = given[i] + more
            spare = spare - more
    return np.array(given)


def noise(own_key, shape, width, limit, cuts=(), kind=jnp.bfloat16):
    entries = width * jax.random.normal(own_key, shape, jnp.float32)
    if cuts:
        entries = entries * steps_of(own_key, shape, cuts, -0.22, 0.18)
    return jnp.clip(entries, -limit, limit).astype(kind)


def setup_inputs(seed: int = 0) -> dict:
    key_of = jax.random.split(jax.random.key(seed), 17)
    hidden_in = noise(key_of[0], (TOKENS, D), 0.5, 3.0, ((0, 32),))
    queries = noise(key_of[1], (TOKENS, D), 1.0, 2.5, ((0, 32),))
    new_keys = noise(key_of[2], (TOKENS, D), 1.0, 2.5, ((0, 32),))
    new_values = noise(key_of[3], (TOKENS, D), 1.5, 6.0, ((0, 32),))
    key_pool = noise(key_of[4], (BLOCKS * POOL, D), 1.0, 2.5, ((0, 32),))
    value_pool = noise(key_of[5], (BLOCKS * POOL, D), 1.5, 6.0, ((0, 32),))
    page_order = jax.vmap(lambda own: jax.random.permutation(own, PAGES_DEV))(jax.random.split(key_of[6], BLOCKS)).reshape((BLOCKS, PAGES_DEV)).astype(jnp.int32)
    new_lengths = jax.vmap(lambda own: uneven_parts(own, REQ_DEV, TOK_DEV, NEW_MOST, 1))(jax.random.split(key_of[7], BLOCKS)).reshape((BLOCKS, REQ_DEV)).astype(jnp.int32)
    context_lengths = jax.vmap(lambda own: uneven_parts(own, REQ_DEV, CTX_TOTAL, CTX_MOST, 2))(jax.random.split(key_of[8], BLOCKS)).reshape((BLOCKS, REQ_DEV)).astype(jnp.int32)
    route_ids_keys = jax.random.split(jax.random.fold_in(key_of[9], 1), TOKENS // TOK_DEV)
    route_ids_turns = jax.random.permutation(jax.random.fold_in(key_of[9], 3), TOKENS // TOK_DEV)
    route_ids = jax.vmap(lambda own, number: shared_out(jax.random.fold_in(key_of[9], 2), own, number, TOK_DEV, EXPERTS, TOP, MOST, 2))(route_ids_keys, route_ids_turns).reshape((TOKENS, TOP))
    norm_gain = jnp.clip(1.0 + 0.15 * jax.random.normal(key_of[10], (D,), jnp.float32), 0.25, 1.75).astype(jnp.bfloat16)
    router_weight = noise(key_of[11], (D, EXPERTS), D ** -0.5, 0.125)
    gate_weight = noise(key_of[12], (EXPERTS, D, FF), D ** -0.5, 0.125, ((0, 4), (2, 8)))
    up_weight = noise(key_of[13], (EXPERTS, D, FF), D ** -0.5, 0.125, ((0, 4), (2, 8)))
    down_weight = noise(key_of[14], (EXPERTS, FF, D), FF ** -0.5, 0.078125, ((0, 4), (1, 8)))
    out_gain = jnp.clip(1.0 + 0.15 * jax.random.normal(key_of[15], (D,), jnp.float32), 0.25, 1.75).astype(jnp.bfloat16)
    return {"hidden_in": hidden_in, "queries": queries, "new_keys": new_keys, "new_values": new_values, "key_pool": key_pool, "value_pool": value_pool, "page_order": page_order, "new_lengths": new_lengths, "context_lengths": context_lengths, "route_ids": route_ids, "norm_gain": norm_gain, "router_weight": router_weight, "gate_weight": gate_weight, "up_weight": up_weight, "down_weight": down_weight, "out_gain": out_gain}


def rms_scale(values, gain):
    mean_square = lax.optimization_barrier(jnp.mean(values * values, axis=-1, keepdims=True))
    return values * lax.rsqrt(mean_square + 1e-05) * gain.astype(jnp.float32)

def route_probs(normed, router_weight, route_ids):
    logits = jnp.dot(normed, router_weight, preferred_element_type=jnp.float32)
    expert_range = jnp.arange(router_weight.shape[1], dtype=jnp.int32)
    picked = lax.optimization_barrier(jnp.sum(jnp.where(route_ids[:, :, None] == expert_range[None, None, :], logits[:, None, :], 0.0), axis=2))
    raised = jnp.exp(picked)
    return raised / lax.optimization_barrier(jnp.sum(raised, axis=1, keepdims=True))

def attend(hidden_rows, query_rows, key_rows, value_rows, key_store, value_store, page_row, new_row_lengths, context_row_lengths):
    row_count = query_rows.shape[0]
    store_count = key_store.shape[0]
    requests = new_row_lengths.shape[0]
    table = page_row.reshape(requests, -1)
    per_request = table.shape[1]
    ends = jnp.cumsum(new_row_lengths).astype(jnp.int32)
    row_index = jnp.arange(row_count, dtype=jnp.int32)
    owner = lax.optimization_barrier(jnp.sum((row_index[:, None] >= ends[None, :]).astype(jnp.int32), axis=1)).astype(jnp.int32)
    request_index = jnp.arange(requests, dtype=jnp.int32)
    row_owner = owner[:, None] == request_index[None, :]
    token_index = jnp.arange(store_count, dtype=jnp.int32)
    token_page = token_index // PAGE
    token_offset = token_index % PAGE
    matched = table[:, :, None] == token_page[None, None, :]
    page_slot = jnp.arange(per_request, dtype=jnp.int32) * PAGE
    position = lax.optimization_barrier(jnp.sum(jnp.where(matched, page_slot[None, :, None], 0), axis=1)).astype(jnp.int32) + token_offset[None, :]
    visible = jnp.any(matched, axis=1) & (position < context_row_lengths[:, None])
    store_mask = jnp.any(row_owner[:, :, None] & visible[None, :, :], axis=1)
    fresh_mask = (owner[:, None] == owner[None, :]) & (row_index[None, :] <= row_index[:, None])
    allowed = jnp.concatenate([store_mask, fresh_mask], axis=1)
    keys = jnp.concatenate([key_store, key_rows], axis=0).reshape(-1, HEADS, HEAD_DIM).astype(jnp.float32)
    values = jnp.concatenate([value_store, value_rows], axis=0).reshape(-1, HEADS, HEAD_DIM).astype(jnp.float32)
    query_heads = query_rows.reshape(row_count, HEADS, HEAD_DIM).astype(jnp.float32)
    scores = jnp.einsum('rhd,khd->hrk', query_heads, keys) * HEAD_DIM ** (-0.5)
    raised = jnp.where(allowed[None, :, :], jnp.exp(scores), 0.0)
    weights = (raised / lax.optimization_barrier(jnp.sum(raised, axis=2, keepdims=True))).astype(jnp.bfloat16)
    attended = jnp.einsum('hrk,khd->rhd', weights.astype(jnp.float32), values).reshape(row_count, HEADS * HEAD_DIM)
    return hidden_rows.astype(jnp.float32) + attended

def reference(hidden_in, queries, new_keys, new_values, key_pool, value_pool, page_order, new_lengths, context_lengths, route_ids, norm_gain, router_weight, gate_weight, up_weight, down_weight, out_gain):

    def one_block(packed):
        return attend(*packed)
    blocked = (hidden_in.reshape(BLOCKS, TOK_DEV, D), queries.reshape(BLOCKS, TOK_DEV, D), new_keys.reshape(BLOCKS, TOK_DEV, D), new_values.reshape(BLOCKS, TOK_DEV, D), key_pool.reshape(BLOCKS, POOL, D), value_pool.reshape(BLOCKS, POOL, D), page_order, new_lengths, context_lengths)
    resid = lax.map(one_block, blocked).reshape(TOKENS, D)
    normed = rms_scale(resid, norm_gain).astype(jnp.bfloat16)
    route_weights = route_probs(normed, router_weight, route_ids)
    mixed = resid
    capacity = BLOCKS * MOST
    for expert in range(EXPERTS):
        chosen = route_ids == expert
        selected = jnp.any(chosen, axis=1)
        count = jnp.sum(selected.astype(jnp.int32)).astype(jnp.int32)
        index = jnp.nonzero(selected, size=capacity, fill_value=0)[0].astype(jnp.int32)
        valid = jnp.arange(capacity, dtype=jnp.int32) < count
        rows_in = normed[index]
        gate_value = jnp.dot(rows_in, gate_weight[expert], preferred_element_type=jnp.float32)
        up_value = jnp.dot(rows_in, up_weight[expert], preferred_element_type=jnp.float32)
        hidden = (jax.nn.silu(gate_value) * up_value).astype(jnp.bfloat16)
        down_expert = down_weight[expert]

        def add_part(part, total):
            start = (part * FF_SLICE).astype(jnp.int32)
            hidden_part = lax.dynamic_slice_in_dim(hidden, start, FF_SLICE, 1)
            down_part = lax.dynamic_slice_in_dim(down_expert, start, FF_SLICE, 0)
            term = jnp.dot(hidden_part, down_part, preferred_element_type=jnp.float32).astype(jnp.bfloat16)
            return total + term.astype(jnp.float32)
        summed = lax.fori_loop(0, N_SH, add_part, jnp.zeros((capacity, D), jnp.float32))
        expert_out = summed.astype(jnp.bfloat16)
        token_weight = lax.optimization_barrier(jnp.sum(jnp.where(chosen, route_weights, 0.0), axis=1))
        scale = jnp.where(valid, token_weight[index], 0.0)
        mixed = mixed.at[index].add(scale[:, None] * expert_out.astype(jnp.float32))
    return rms_scale(mixed, out_gain).astype(jnp.bfloat16)
```

```python
import functools
import jax
import jax.numpy as jnp
from jax import lax
from jax.experimental import pallas as pl
from jax.experimental.pallas import tpu as pltpu
from jax.sharding import PartitionSpec as P

HEAD_DIM = 64
PAGE = 16
MOST = 32
BF = jnp.bfloat16
F32 = jnp.float32
MESH = pl.DeviceIdType.MESH


def dot(a, b):
    return jnp.dot(a, b, preferred_element_type=F32)


def dot_nt(a, b):
    return lax.dot_general(a, b, (((1,), (1,)), ((), ())), preferred_element_type=F32)


def dot_tn(a, b):
    return lax.dot_general(a, b, (((0,), (0,)), ((), ())), preferred_element_type=F32)


def attend_kernel(
    new_len, ctx_len, page, ids, hid, q, kn, vn, kp, vp, gain, router,
    resid, outgoing, u_high, u_low, pool_bias, new_bias,
):
    step = pl.program_id(0)
    rows = q.shape[0]
    store = kp.shape[0]
    requests = new_len.shape[1]
    entries = page.shape[0]
    per_request = entries // requests

    @pl.when(step == 0)
    def _():
        token = lax.broadcasted_iota(jnp.int32, (entries, store), 1)
        entry = lax.broadcasted_iota(jnp.int32, (entries, store), 0)
        place = jnp.sum(
            jnp.where(page[...] == token // PAGE, entry, 0), axis=0, keepdims=True
        )
        offset = lax.broadcasted_iota(jnp.int32, (1, store), 1) % PAGE
        row_at = lax.broadcasted_iota(jnp.int32, (rows, 1), 0)
        col_at = lax.broadcasted_iota(jnp.int32, (1, rows), 1)
        row_owner = jnp.zeros((rows, 1), jnp.int32)
        col_owner = jnp.zeros((1, rows), jnp.int32)
        token_owner = place // per_request
        position = (place % per_request) * PAGE + offset
        limit = jnp.zeros((1, store), jnp.int32)
        end = 0
        for r in range(requests):
            end = end + new_len[0, r]
            row_owner += (row_at >= end).astype(jnp.int32)
            col_owner += (col_at >= end).astype(jnp.int32)
            limit += jnp.where(token_owner == r, ctx_len[0, r], 0)
        token_owner = jnp.where(position < limit, token_owner, -1)
        pool_bias[...] = jnp.where(row_owner == token_owner, 0.0, -1e30)
        new_bias[...] = jnp.where(
            (row_owner == col_owner) & (col_at <= row_at), 0.0, -1e30
        )

    lane = lax.broadcasted_iota(jnp.int32, (rows, 2 * HEAD_DIM), 1)
    first = lane < HEAD_DIM
    query = q[...].astype(F32) * (HEAD_DIM ** -0.5)
    zero = jnp.zeros_like(query)
    q_heads = (jnp.where(first, query, zero).astype(BF), jnp.where(first, zero, query).astype(BF))
    keys, fresh = kp[...], kn[...]
    vals, fresh_vals = vp[...], vn[...]
    results = []
    for qh in q_heads:
        raised = jnp.exp(dot_nt(qh, keys) + pool_bias[...])
        raised_new = jnp.exp(dot_nt(qh, fresh) + new_bias[...])
        total = jnp.sum(raised, axis=1, keepdims=True) + jnp.sum(
            raised_new, axis=1, keepdims=True
        )
        result = dot(raised.astype(BF), vals) + dot(raised_new.astype(BF), fresh_vals)
        results.append(result / total)
    columns = pl.ds(pl.multiple_of(step * 2 * HEAD_DIM, 2 * HEAD_DIM), 2 * HEAD_DIM)
    resid[:, columns] = hid[...].astype(F32) + jnp.where(first, results[0], results[1])

    @pl.when(step == pl.num_programs(0) - 1)
    def _():
        values = resid[...]
        mean_square = jnp.mean(values * values, axis=1, keepdims=True)
        normed = (
            values * lax.rsqrt(mean_square + 1e-05) * gain[...].astype(F32)
        ).astype(BF)
        logits = dot(normed, router[...])
        experts = router.shape[1]
        expert_at = lax.broadcasted_iota(jnp.int32, (rows, experts), 1)
        slots = experts * MOST
        slot_at = lax.broadcasted_iota(jnp.int32, (rows, slots), 1)
        slot_expert = slot_at // MOST
        raised = []
        for k in range(ids.shape[1]):
            named = ids[:, k : k + 1]
            raised.append(
                jnp.exp(
                    jnp.sum(
                        jnp.where(expert_at == named, logits, 0.0), axis=1, keepdims=True
                    )
                )
            )
        total = sum(raised)
        weight = jnp.zeros((rows, slots), F32)
        chosen = jnp.zeros((rows, slots), F32)
        for k in range(ids.shape[1]):
            named = ids[:, k : k + 1] == slot_expert
            weight += jnp.where(named, raised[k] / total, 0.0)
            chosen += jnp.where(named, 1.0, 0.0)
        r_at = lax.broadcasted_iota(jnp.int32, (rows, rows), 0)
        c_at = lax.broadcasted_iota(jnp.int32, (rows, rows), 1)
        before = dot(jnp.where(c_at < r_at, 1.0, 0.0).astype(BF), chosen.astype(BF))
        taken = (chosen > 0.5) & (before.astype(jnp.int32) == slot_at % MOST)
        weight = jnp.where(taken, weight, 0.0)
        high = weight.astype(BF)
        u_high[...] = high
        u_low[...] = (weight - high.astype(F32)).astype(BF)
        outgoing[...] = dot_tn(jnp.where(taken, 1.0, 0.0).astype(BF), normed).astype(BF)


def attend(new_len, ctx_len, page, ids, hid, q, kn, vn, kp, vp, gain, router):
    rows, width = q.shape
    store = kp.shape[0]
    slots = router.shape[1] * MOST
    pair = 2 * HEAD_DIM
    smem = pl.BlockSpec(memory_space=pltpu.SMEM)

    def whole(shape):
        return pl.BlockSpec(shape, lambda i: (0, 0))

    def head(count):
        return pl.BlockSpec((count, pair), lambda i: (0, i))

    return pl.pallas_call(
        attend_kernel,
        grid=(width // pair,),
        in_specs=[
            smem, smem, whole(page.shape), whole(ids.shape), head(rows), head(rows),
            head(rows), head(rows), head(store), head(store), whole(gain.shape),
            whole(router.shape),
        ],
        out_specs=[
            whole((rows, width)), whole((slots, width)), whole((rows, slots)),
            whole((rows, slots)),
        ],
        out_shape=[
            jax.ShapeDtypeStruct((rows, width), F32),
            jax.ShapeDtypeStruct((slots, width), BF),
            jax.ShapeDtypeStruct((rows, slots), BF),
            jax.ShapeDtypeStruct((rows, slots), BF),
        ],
        scratch_shapes=[pltpu.VMEM((rows, store), F32), pltpu.VMEM((rows, rows), F32)],
        compiler_params=pltpu.CompilerParams(vmem_limit_bytes=40 * 2**20),
    )(new_len, ctx_len, page, ids, hid, q, kn, vn, kp, vp, gain, router)


def expert_kernel(
    groups, members,
    outgoing, gate, up, down, resid, u_high, u_low, gain, out,
    gath, sums, ret, gate_v, up_v, down_v, hidden,
    own_sem, weight_sem, to_send, to_recv, ag_send, ag_recv, rs_send, rs_recv,
    back_send, back_recv,
):
    local = gate.shape[0]
    width = gate.shape[1]
    ff = gate.shape[2]
    bits = members.bit_length() - 1
    group = lax.axis_index("ex")
    member = lax.axis_index("sh")
    flips = []
    for d in range(bits):
        b = members >> (d + 1)
        flips.append(member + b - 2 * b * ((member // b) % 2))
    orders = [
        [1, 0] + list(range(2, bits)) if e % 2 == 0 and bits > 1 else list(range(bits))
        for e in range(local)
    ]

    barrier = pltpu.get_barrier_semaphore()
    for d in range(bits):
        pl.semaphore_signal(barrier, inc=1, device_id=(group, flips[d]), device_id_type=MESH)
    for k in range(1, groups):
        pl.semaphore_signal(
            barrier, inc=1, device_id=((group + k) % groups, member), device_id_type=MESH
        )

    own = pltpu.make_async_copy(
        outgoing.at[group], gath.at[(0, slice(None)) + (0,) * bits], own_sem
    )
    own.start()
    weight_copies = [
        pltpu.make_async_copy(src, dst, weight_sem.at[i])
        for i, (src, dst) in enumerate(((gate, gate_v), (up, up_v), (down, down_v)))
    ]
    pl.semaphore_wait(barrier, bits + groups - 1)

    def to_copy(k):
        return pltpu.make_async_remote_copy(
            src_ref=outgoing.at[(group + k) % groups],
            dst_ref=gath.at[(k, slice(None)) + (0,) * bits],
            send_sem=to_send.at[k],
            recv_sem=to_recv.at[k],
            device_id=((group + k) % groups, member),
            device_id_type=MESH,
        )

    def back_copy(k):
        return pltpu.make_async_remote_copy(
            src_ref=gath.at[(k, slice(None)) + (0,) * bits],
            dst_ref=ret.at[group],
            send_sem=back_send.at[k],
            recv_sem=back_recv.at[k],
            device_id=((group - k + groups) % groups, member),
            device_id_type=MESH,
        )

    def index(k, e, every, d, value):
        return (k, e) + tuple(
            slice(None) if x in every else (value if x == d else 0) for x in range(bits)
        )

    def ag_copy(k, e, j):
        d, every = orders[e][j], orders[e][:j]
        return pltpu.make_async_remote_copy(
            src_ref=gath.at[index(k, e, every, d, 0)],
            dst_ref=gath.at[index(k, e, every, d, 1)],
            send_sem=ag_send.at[k, e, j],
            recv_sem=ag_recv.at[k, e, j],
            device_id=(group, flips[d]),
            device_id_type=MESH,
        )

    def rs_copy(k, e, j):
        d, every = orders[e][bits - 1 - j], orders[e][: bits - 1 - j]
        return pltpu.make_async_remote_copy(
            src_ref=gath.at[index(k, e, every, d, 1)],
            dst_ref=sums.at[index(k, e, every, d, 1)],
            send_sem=rs_send.at[k, e, j],
            recv_sem=rs_recv.at[k, e, j],
            device_id=(group, flips[d]),
            device_id_type=MESH,
        )

    def rs_add(k, e, j):
        d, every = orders[e][bits - 1 - j], orders[e][: bits - 1 - j]
        kept, came = index(k, e, every, d, 0), index(k, e, every, d, 1)
        gath[kept] = (gath[kept].astype(F32) + sums[came].astype(F32)).astype(BF)

    for k in range(1, groups):
        to_copy(k).start()
    for copy in weight_copies:
        copy.start()
    own.wait()

    def feed(k, e):
        ag_copy(k, e, bits - 1).wait_recv()
        rows = gath[k, e].reshape(members * MOST, width)
        for at in range(0, ff, 256):
            size = min(256, ff - at)
            gate_value = dot(rows, gate_v[e, :, at : at + size])
            up_value = dot(rows, up_v[e, :, at : at + size])
            hidden[:, at : at + size] = (
                gate_value / (1.0 + jnp.exp(-gate_value)) * up_value
            ).astype(BF)
        for j in range(bits):
            ag_copy(k, e, j).wait_send()
        units = hidden[...]
        for at in range(0, width, 256):
            size = min(256, width - at)
            part = dot(units, down_v[e, :, at : at + size]).astype(BF)
            gath[k, e, ..., at : at + size] = part.reshape(
                (2,) * bits + (MOST, size)
            )

    def within(k):
        return (k >= 0) & (k < groups)

    def turn(i, carry):
        k = i - bits
        for j in range(bits):
            s = k + bits - j

            @pl.when(within(s))
            def _(s=s, j=j):
                if j == 0:
                    @pl.when(s >= 1)
                    def _():
                        to_copy(s).wait_recv()

                for e in range(local):
                    if j > 0:
                        ag_copy(s, e, j - 1).wait_recv()
                    ag_copy(s, e, j).start()

        @pl.when(k == 0)
        def _():
            for copy in weight_copies:
                copy.wait()

        def reduce_step(j):
            s = k - j

            @pl.when(within(s))
            def _():
                for e in range(local):
                    rs_copy(s, e, j - 1).wait_recv()
                    rs_add(s, e, j - 1)
                    if j < bits:
                        rs_copy(s, e, j).start()
                if j == bits:
                    @pl.when(s >= 1)
                    def _():
                        back_copy(s).start()

        for j in range(bits, 1, -1):
            reduce_step(j)
        for e in range(local):
            @pl.when(within(k))
            def _(e=e):
                feed(k, e)
                rs_copy(k, e, 0).start()

            if e == 0:
                reduce_step(1)
        return carry

    lax.fori_loop(0, groups + 2 * bits, turn, 0)
    ret[group] = gath[(0, slice(None)) + (0,) * bits]

    def finish(k, carry):
        for e in range(local):
            for j in range(bits):
                rs_copy(k, e, j).wait_send()

        @pl.when(k >= 1)
        def _():
            to_copy(k).wait_send()
            back_copy(k).wait()

        return carry

    lax.fori_loop(0, groups, finish, 0)
    came = ret[...].reshape(groups * local * MOST, width)
    mixed = resid[...] + dot(u_high[...], came) + dot(u_low[...], came)
    mean_square = jnp.mean(mixed * mixed, axis=1, keepdims=True)
    out[...] = (mixed * lax.rsqrt(mean_square + 1e-05) * gain[...].astype(F32)).astype(BF)


def experts(groups, members, outgoing, gate, up, down, resid, u_high, u_low, gain):
    local, width, ff = gate.shape
    bits = members.bit_length() - 1
    any_spec = pl.BlockSpec(memory_space=pl.ANY)
    vmem = pl.BlockSpec(memory_space=pltpu.VMEM)
    block = (groups, local) + (2,) * bits + (MOST, width)
    dma = pltpu.SemaphoreType.DMA
    return pl.pallas_call(
        functools.partial(expert_kernel, groups, members),
        in_specs=[any_spec] * 4 + [vmem] * 4,
        out_specs=vmem,
        out_shape=jax.ShapeDtypeStruct(resid.shape, BF),
        scratch_shapes=[
            pltpu.VMEM(block, BF),
            pltpu.VMEM(block, BF),
            pltpu.VMEM((groups, local, MOST, width), BF),
            pltpu.VMEM(gate.shape, BF),
            pltpu.VMEM(up.shape, BF),
            pltpu.VMEM(down.shape, BF),
            pltpu.VMEM((members * MOST, ff), BF),
            dma,
            dma((3,)),
            dma((groups,)),
            dma((groups,)),
            dma((groups, local, bits)),
            dma((groups, local, bits)),
            dma((groups, local, bits)),
            dma((groups, local, bits)),
            dma((groups,)),
            dma((groups,)),
        ],
        compiler_params=pltpu.CompilerParams(
            collective_id=0, has_side_effects=True, vmem_limit_bytes=62 * 2**20
        ),
    )(
        outgoing.reshape(groups, local, MOST, width), gate, up, down, resid, u_high, u_low, gain
    )


def per_device(
    groups,
    members,
    hidden_in,
    queries,
    new_keys,
    new_values,
    key_pool,
    value_pool,
    page_order,
    new_lengths,
    context_lengths,
    route_ids,
    norm_gain,
    router_weight,
    gate_weight,
    up_weight,
    down_weight,
    out_gain,
):
    resid, outgoing, u_high, u_low = attend(
        new_lengths,
        context_lengths,
        page_order.reshape(-1, 1),
        route_ids,
        hidden_in,
        queries,
        new_keys,
        new_values,
        key_pool,
        value_pool,
        norm_gain.reshape(1, -1),
        router_weight,
    )
    return experts(
        groups, members, outgoing, gate_weight, up_weight, down_weight, resid, u_high, u_low,
        out_gain.reshape(1, -1),
    )


def solution(mesh):
    placed = (P(("ex", "sh"), None),) * 10 + (
        P(),
        P(),
        P("ex", None, "sh"),
        P("ex", None, "sh"),
        P("ex", "sh", None),
        P(),
    )
    return jax.shard_map(
        functools.partial(per_device, mesh.shape["ex"], mesh.shape["sh"]),
        mesh=mesh,
        in_specs=placed,
        out_specs=P(("ex", "sh"), None),
        check_vma=False,
    )
```

```python
import functools
import jax
import jax.numpy as jnp
from jax import lax
from jax.experimental import pallas as pl
from jax.experimental.pallas import tpu as pltpu
from jax.sharding import PartitionSpec as P

HEAD_DIM = 64
PAGE = 16
MOST = 32
BF = jnp.bfloat16
F32 = jnp.float32
MESH = pl.DeviceIdType.MESH


def dot(a, b):
    return jnp.dot(a, b, preferred_element_type=F32)


def dot_nt(a, b):
    return lax.dot_general(a, b, (((1,), (1,)), ((), ())), preferred_element_type=F32)


def dot_tn(a, b):
    return lax.dot_general(a, b, (((0,), (0,)), ((), ())), preferred_element_type=F32)


def attend_kernel(
    new_len, ctx_len, page, ids, hid, q, kn, vn, kp, vp, gain, router,
    resid, outgoing, u_high, u_low, pool_bias, new_bias,
):
    step = pl.program_id(0)
    rows = q.shape[0]
    store = kp.shape[0]
    requests = new_len.shape[1]
    entries = page.shape[0]
    per_request = entries // requests

    @pl.when(step == 0)
    def _():
        token = lax.broadcasted_iota(jnp.int32, (entries, store), 1)
        entry = lax.broadcasted_iota(jnp.int32, (entries, store), 0)
        place = jnp.sum(
            jnp.where(page[...] == token // PAGE, entry, 0), axis=0, keepdims=True
        )
        offset = lax.broadcasted_iota(jnp.int32, (1, store), 1) % PAGE
        row_at = lax.broadcasted_iota(jnp.int32, (rows, 1), 0)
        col_at = lax.broadcasted_iota(jnp.int32, (1, rows), 1)
        row_owner = jnp.zeros((rows, 1), jnp.int32)
        col_owner = jnp.zeros((1, rows), jnp.int32)
        token_owner = place // per_request
        position = (place % per_request) * PAGE + offset
        limit = jnp.zeros((1, store), jnp.int32)
        end = 0
        for r in range(requests):
            end = end + new_len[0, r]
            row_owner += (row_at >= end).astype(jnp.int32)
            col_owner += (col_at >= end).astype(jnp.int32)
            limit += jnp.where(token_owner == r, ctx_len[0, r], 0)
        token_owner = jnp.where(position < limit, token_owner, -1)
        pool_bias[...] = jnp.where(row_owner == token_owner, 0.0, -1e30)
        new_bias[...] = jnp.where(
            (row_owner == col_owner) & (col_at <= row_at), 0.0, -1e30
        )

    lane = lax.broadcasted_iota(jnp.int32, (rows, 2 * HEAD_DIM), 1)
    first = lane < HEAD_DIM
    query = q[...].astype(F32) * (HEAD_DIM ** -0.5)
    zero = jnp.zeros_like(query)
    q_heads = (jnp.where(first, query, zero).astype(BF), jnp.where(first, zero, query).astype(BF))
    keys, fresh = kp[...], kn[...]
    vals, fresh_vals = vp[...], vn[...]
    results = []
    for qh in q_heads:
        raised = jnp.exp(dot_nt(qh, keys) + pool_bias[...])
        raised_new = jnp.exp(dot_nt(qh, fresh) + new_bias[...])
        total = jnp.sum(raised, axis=1, keepdims=True) + jnp.sum(
            raised_new, axis=1, keepdims=True
        )
        result = dot(raised.astype(BF), vals) + dot(raised_new.astype(BF), fresh_vals)
        results.append(result / total)
    columns = pl.ds(pl.multiple_of(step * 2 * HEAD_DIM, 2 * HEAD_DIM), 2 * HEAD_DIM)
    resid[:, columns] = hid[...].astype(F32) + jnp.where(first, results[0], results[1])

    @pl.when(step == pl.num_programs(0) - 1)
    def _():
        values = resid[...]
        mean_square = jnp.mean(values * values, axis=1, keepdims=True)
        normed = (
            values * lax.rsqrt(mean_square + 1e-05) * gain[...].astype(F32)
        ).astype(BF)
        logits = dot_nt(normed, router[...])
        experts = router.shape[0]
        expert_at = lax.broadcasted_iota(jnp.int32, (rows, experts), 1)
        slots = experts * MOST
        slot_at = lax.broadcasted_iota(jnp.int32, (rows, slots), 1)
        slot_expert = slot_at // MOST
        raised = []
        for k in range(ids.shape[1]):
            named = ids[:, k : k + 1]
            raised.append(
                jnp.exp(
                    jnp.sum(
                        jnp.where(expert_at == named, logits, 0.0), axis=1, keepdims=True
                    )
                )
            )
        total = sum(raised)
        weight = jnp.zeros((rows, slots), F32)
        chosen = jnp.zeros((rows, slots), F32)
        for k in range(ids.shape[1]):
            named = ids[:, k : k + 1] == slot_expert
            weight += jnp.where(named, raised[k] / total, 0.0)
            chosen += jnp.where(named, 1.0, 0.0)
        r_at = lax.broadcasted_iota(jnp.int32, (rows, rows), 0)
        c_at = lax.broadcasted_iota(jnp.int32, (rows, rows), 1)
        before = dot(jnp.where(c_at < r_at, 1.0, 0.0).astype(BF), chosen.astype(BF))
        taken = (chosen > 0.5) & (before.astype(jnp.int32) == slot_at % MOST)
        weight = jnp.where(taken, weight, 0.0)
        high = weight.astype(BF)
        u_high[...] = high
        u_low[...] = (weight - high.astype(F32)).astype(BF)
        outgoing[...] = dot_tn(jnp.where(taken, 1.0, 0.0).astype(BF), normed).astype(BF)


def attend(new_len, ctx_len, page, ids, hid, q, kn, vn, kp, vp, gain, router):
    rows, width = q.shape
    store = kp.shape[0]
    slots = router.shape[0] * MOST
    pair = 2 * HEAD_DIM
    smem = pl.BlockSpec(memory_space=pltpu.SMEM)

    def whole(shape):
        return pl.BlockSpec(shape, lambda i: (0, 0))

    def head(count):
        return pl.BlockSpec((count, pair), lambda i: (0, i))

    return pl.pallas_call(
        attend_kernel,
        grid=(width // pair,),
        in_specs=[
            smem, smem, whole(page.shape), whole(ids.shape), head(rows), head(rows),
            head(rows), head(rows), head(store), head(store), whole(gain.shape),
            whole(router.shape),
        ],
        out_specs=[
            whole((rows, width)), whole((slots, width)), whole((rows, slots)),
            whole((rows, slots)),
        ],
        out_shape=[
            jax.ShapeDtypeStruct((rows, width), F32),
            jax.ShapeDtypeStruct((slots, width), BF),
            jax.ShapeDtypeStruct((rows, slots), BF),
            jax.ShapeDtypeStruct((rows, slots), BF),
        ],
        scratch_shapes=[pltpu.VMEM((rows, store), F32), pltpu.VMEM((rows, rows), F32)],
        compiler_params=pltpu.CompilerParams(vmem_limit_bytes=62 * 2**20),
    )(new_len, ctx_len, page, ids, hid, q, kn, vn, kp, vp, gain, router)


def expert_kernel(
    groups, members,
    outgoing, gate, up, down, resid, u_high, u_low, gain, out,
    gath, sums, ret, gate_v, up_v, down_v, hidden,
    own_sem, weight_sem, to_send, to_recv, ag_send, ag_recv, rs_send, rs_recv,
    back_send, back_recv,
):
    local = gate.shape[0]
    ff = gate.shape[1]
    width = gate.shape[2]
    bits = members.bit_length() - 1
    group = lax.axis_index("ex")
    member = lax.axis_index("sh")
    flips = []
    for d in range(bits):
        b = members >> (d + 1)
        flips.append(member + b - 2 * b * ((member // b) % 2))
    orders = [
        [1, 0] + list(range(2, bits)) if e % 2 == 0 and bits > 1 else list(range(bits))
        for e in range(local)
    ]

    barrier = pltpu.get_barrier_semaphore()
    for d in range(bits):
        pl.semaphore_signal(barrier, inc=1, device_id=(group, flips[d]), device_id_type=MESH)
    for k in range(1, groups):
        pl.semaphore_signal(
            barrier, inc=1, device_id=((group + k) % groups, member), device_id_type=MESH
        )

    own = pltpu.make_async_copy(
        outgoing.at[group], gath.at[(0, slice(None)) + (0,) * bits], own_sem
    )
    own.start()
    weight_copies = [
        pltpu.make_async_copy(src, dst, weight_sem.at[i])
        for i, (src, dst) in enumerate(((gate, gate_v), (up, up_v), (down, down_v)))
    ]
    pl.semaphore_wait(barrier, bits + groups - 1)

    def to_copy(k):
        return pltpu.make_async_remote_copy(
            src_ref=outgoing.at[(group + k) % groups],
            dst_ref=gath.at[(k, slice(None)) + (0,) * bits],
            send_sem=to_send.at[k],
            recv_sem=to_recv.at[k],
            device_id=((group + k) % groups, member),
            device_id_type=MESH,
        )

    def back_copy(k):
        return pltpu.make_async_remote_copy(
            src_ref=gath.at[(k, slice(None)) + (0,) * bits],
            dst_ref=ret.at[group],
            send_sem=back_send.at[k],
            recv_sem=back_recv.at[k],
            device_id=((group - k + groups) % groups, member),
            device_id_type=MESH,
        )

    def index(k, e, every, d, value):
        return (k, e) + tuple(
            slice(None) if x in every else (value if x == d else 0) for x in range(bits)
        )

    def ag_copy(k, e, j):
        d, every = orders[e][j], orders[e][:j]
        return pltpu.make_async_remote_copy(
            src_ref=gath.at[index(k, e, every, d, 0)],
            dst_ref=gath.at[index(k, e, every, d, 1)],
            send_sem=ag_send.at[k, e, j],
            recv_sem=ag_recv.at[k, e, j],
            device_id=(group, flips[d]),
            device_id_type=MESH,
        )

    def rs_copy(k, e, j):
        d, every = orders[e][bits - 1 - j], orders[e][: bits - 1 - j]
        return pltpu.make_async_remote_copy(
            src_ref=gath.at[index(k, e, every, d, 1)],
            dst_ref=sums.at[index(k, e, every, d, 1)],
            send_sem=rs_send.at[k, e, j],
            recv_sem=rs_recv.at[k, e, j],
            device_id=(group, flips[d]),
            device_id_type=MESH,
        )

    def rs_add(k, e, j):
        d, every = orders[e][bits - 1 - j], orders[e][: bits - 1 - j]
        kept, came = index(k, e, every, d, 0), index(k, e, every, d, 1)
        gath[kept] = (gath[kept].astype(F32) + sums[came].astype(F32)).astype(BF)

    for k in range(1, groups):
        to_copy(k).start()
    for copy in weight_copies:
        copy.start()
    own.wait()

    def feed(k, e):
        ag_copy(k, e, bits - 1).wait_recv()
        rows = gath[k, e].reshape(members * MOST, width)
        for at in range(0, ff, 256):
            size = min(256, ff - at)
            gate_value = dot_nt(rows, gate_v[e, at : at + size, :])
            up_value = dot_nt(rows, up_v[e, at : at + size, :])
            hidden[:, at : at + size] = (
                gate_value / (1.0 + jnp.exp(-gate_value)) * up_value
            ).astype(BF)
        for j in range(bits):
            ag_copy(k, e, j).wait_send()
        units = hidden[...]
        for at in range(0, width, 256):
            size = min(256, width - at)
            part = dot(units, down_v[e, :, at : at + size]).astype(BF)
            gath[k, e, ..., at : at + size] = part.reshape(
                (2,) * bits + (MOST, size)
            )

    def within(k):
        return (k >= 0) & (k < groups)

    def turn(i, carry):
        k = i - bits
        for j in range(bits):
            s = k + bits - j

            @pl.when(within(s))
            def _(s=s, j=j):
                if j == 0:
                    @pl.when(s >= 1)
                    def _():
                        to_copy(s).wait_recv()

                for e in range(local):
                    if j > 0:
                        ag_copy(s, e, j - 1).wait_recv()
                    ag_copy(s, e, j).start()

        @pl.when(k == 0)
        def _():
            for copy in weight_copies:
                copy.wait()

        def reduce_step(j):
            s = k - j

            @pl.when(within(s))
            def _():
                for e in range(local):
                    rs_copy(s, e, j - 1).wait_recv()
                    rs_add(s, e, j - 1)
                    if j < bits:
                        rs_copy(s, e, j).start()
                if j == bits:
                    @pl.when(s >= 1)
                    def _():
                        back_copy(s).start()

        for j in range(bits, 1, -1):
            reduce_step(j)
        for e in range(local):
            @pl.when(within(k))
            def _(e=e):
                feed(k, e)
                rs_copy(k, e, 0).start()

            if e == 0:
                reduce_step(1)
        return carry

    lax.fori_loop(0, groups + 2 * bits, turn, 0)
    ret[group] = gath[(0, slice(None)) + (0,) * bits]

    def finish(k, carry):
        for e in range(local):
            for j in range(bits):
                rs_copy(k, e, j).wait_send()

        @pl.when(k >= 1)
        def _():
            to_copy(k).wait_send()
            back_copy(k).wait()

        return carry

    lax.fori_loop(0, groups, finish, 0)
    came = ret[...].reshape(groups * local * MOST, width)
    mixed = resid[...] + dot(u_high[...], came) + dot(u_low[...], came)
    mean_square = jnp.mean(mixed * mixed, axis=1, keepdims=True)
    out[...] = (mixed * lax.rsqrt(mean_square + 1e-05) * gain[...].astype(F32)).astype(BF)


def experts(groups, members, outgoing, gate, up, down, resid, u_high, u_low, gain):
    local, ff, width = gate.shape
    bits = members.bit_length() - 1
    any_spec = pl.BlockSpec(memory_space=pl.ANY)
    vmem = pl.BlockSpec(memory_space=pltpu.VMEM)
    block = (groups, local) + (2,) * bits + (MOST, width)
    dma = pltpu.SemaphoreType.DMA
    return pl.pallas_call(
        functools.partial(expert_kernel, groups, members),
        in_specs=[any_spec] * 4 + [vmem] * 4,
        out_specs=vmem,
        out_shape=jax.ShapeDtypeStruct(resid.shape, BF),
        scratch_shapes=[
            pltpu.VMEM(block, BF),
            pltpu.VMEM(block, BF),
            pltpu.VMEM((groups, local, MOST, width), BF),
            pltpu.VMEM(gate.shape, BF),
            pltpu.VMEM(up.shape, BF),
            pltpu.VMEM(down.shape, BF),
            pltpu.VMEM((members * MOST, ff), BF),
            dma,
            dma((3,)),
            dma((groups,)),
            dma((groups,)),
            dma((groups, local, bits)),
            dma((groups, local, bits)),
            dma((groups, local, bits)),
            dma((groups, local, bits)),
            dma((groups,)),
            dma((groups,)),
        ],
        compiler_params=pltpu.CompilerParams(
            collective_id=0, has_side_effects=True, vmem_limit_bytes=62 * 2**20
        ),
    )(
        outgoing.reshape(groups, local, MOST, width), gate, up, down, resid, u_high, u_low, gain
    )


def per_device(
    groups,
    members,
    hidden_in,
    queries,
    new_keys,
    new_values,
    key_pool,
    value_pool,
    page_order,
    new_lengths,
    context_lengths,
    route_ids,
    norm_gain,
    router_weight,
    gate_weight,
    up_weight,
    down_weight,
    out_gain,
):
    resid, outgoing, u_high, u_low = attend(
        new_lengths,
        context_lengths,
        page_order.reshape(-1, 1),
        route_ids,
        hidden_in,
        queries,
        new_keys,
        new_values,
        key_pool,
        value_pool,
        norm_gain.reshape(1, -1),
        router_weight.T,
    )
    return experts(
        groups, members, outgoing, gate_weight.transpose(0, 2, 1), up_weight.transpose(0, 2, 1),
        down_weight, resid, u_high, u_low,
        out_gain.reshape(1, -1),
    )


def solution(mesh):
    placed = (P(("ex", "sh"), None),) * 10 + (
        P(),
        P(),
        P("ex", None, "sh"),
        P("ex", None, "sh"),
        P("ex", "sh", None),
        P(),
    )
    return jax.shard_map(
        functools.partial(per_device, mesh.shape["ex"], mesh.shape["sh"]),
        mesh=mesh,
        in_specs=placed,
        out_specs=P(("ex", "sh"), None),
        check_vma=False,
    )
```
